32 devices in a mesh: section: 4 (over y, x), ctx: 8 (over z, core).
Axes of the slice: x: 2, y: 2, z: 4, core: 2. Of those that a mesh axis runs over, the one named last changes fastest.
Arguments:
- queries: bfloat16 [4, 1024, 2048], P('section', 'ctx'), may hold values from -6 to 6
- key_states: bfloat16 [4, 1024, 2048], P('section', 'ctx'), may hold values from -6 to 6
- value_states: bfloat16 [4, 1024, 2048], P('section', 'ctx'), may hold values from -6 to 6
- upstream: bfloat16 [4, 1024, 2048], P('section', 'ctx'), may hold values from -6 to 6
- layout: int32 [4, 16, 8, 4], P('section', 'ctx'), may hold values from 0 to 7, as said below
- segments: int32 [4, 8], P('section'), may hold values from 0 to 2, never falling along the last dimension, each value on 1 to 4 neighbouring positions
Outputs:
- attended: bfloat16 [4, 1024, 2048], P('section', 'ctx')
- grad_queries: bfloat16 [4, 1024, 2048], P('section', 'ctx')
- grad_keys: bfloat16 [4, 1024, 2048], P('section', 'ctx')
- grad_values: bfloat16 [4, 1024, 2048], P('section', 'ctx')
The draws below stay inside these ranges and needn't reach their ends.
Inputs may be any that keep to these rules, and one draw needn't show every extreme that they name: `layout`: for section s, head h and query block a the four entries are a, a - 1, a - 2 and a - 3 - r for some r from 0 to 4, each taken modulo 8; they are distinct.
All inputs are finite; a program needn't handle non-finite values.
Results may differ from the reference program's by a relative error of at most 0.04.
Values may be sent and summed in bfloat16 or wider, within the bound.
A program may use at most 64 MiB of HBM per device.

```python
import math
import jax
import jax.numpy as jnp
import numpy as np
from jax import lax

HEADS = 16
DH = 128
BLK = 128
TOKENS = 1024
NB = 8
SECTIONS = 4


def base_field(key, salt):
    field_key = jax.random.fold_in(key, salt)
    field_shape = (SECTIONS, NB, BLK, HEADS * DH)
    field = jnp.clip(jax.random.normal(field_key, field_shape, jnp.float32), -6.0, 6.0)
    return field


def draw_queries(key, part):
    field = base_field(key, 1)
    return field.reshape(SECTIONS, NB * BLK, HEADS * DH).astype(jnp.bfloat16)


def draw_key_states(key, part):
    field = base_field(key, 2)
    return field.reshape(SECTIONS, NB * BLK, HEADS * DH).astype(jnp.bfloat16)


def draw_layout(key, part):
    stride = jax.random.randint(jax.random.fold_in(key, 7), (SECTIONS, HEADS, NB, 1), 0, NB - 3)
    current = jnp.broadcast_to(jnp.arange(NB).reshape(1, 1, NB, 1), stride.shape)
    slot_blocks = jnp.concatenate([current, current - 1, current - 2, current - 3 - stride], axis=3)
    return jnp.mod(slot_blocks, NB).astype(jnp.int32)


def steps_of(key, extent, cuts, low, largest):
    level = 1.0
    for dim, shards_of in cuts:
        steps = jax.random.uniform(jax.random.fold_in(jax.random.fold_in(key, 6), dim), (shards_of,), jnp.float32, low / len(cuts), largest / len(cuts))
        level = level * jnp.repeat(jnp.exp(steps), extent[dim] // shards_of).reshape((-1,) + (1,) * (len(extent) - 1 - dim))
    return level


def length_profile(count, total, reach, skew):
    portions = [(1 << 20) // math.isqrt(rank ** skew) + 1 for rank in range(2, count + 1)]
    rest, counts = total - reach - (count - 1), [1] * (count - 1)
    while rest > 0:
        movable = [i for i in range(count - 1) if counts[i] < reach]
        whole, remaining = sum([portions[i] for i in movable]), rest
        for i in movable:
            extra = min(reach - counts[i], max(1, remaining * portions[i] // whole), rest)
            counts[i] = counts[i] + extra
            rest = rest - extra
    return np.array([reach] + counts)


def uneven(stream_key, count, total, reach, slope):
    if count == 2:
        one = jax.random.randint(stream_key, (), max(1, total - reach), min(reach, total - 1) + 1)
        return jnp.stack([one, total - one])
    tallies = jnp.asarray(length_profile(count, total, reach, slope), jnp.int32)
    couples = (count - 1) // 2
    source_of, receiver = tallies[1:1 + 2 * couples:2], tallies[2:2 + 2 * couples:2]
    room = jnp.minimum(source_of - 1, reach - receiver)
    passed = jax.random.randint(jax.random.fold_in(stream_key, 1), (couples,), 0, 1 << 20) % (room + 1)
    tallies = tallies.at[1:1 + 2 * couples:2].set(source_of - passed).at[2:2 + 2 * couples:2].set(receiver + passed)
    return tallies[jax.random.permutation(jax.random.fold_in(stream_key, 2), count)]


def noise(own_key, dims, width, most, shards=(), kind=jnp.bfloat16):
    values = width * jax.random.normal(own_key, dims, jnp.float32)
    if shards:
        values = values * steps_of(own_key, dims, shards, -0.22, 0.18)
    return jnp.clip(values, -most, most).astype(kind)


def setup_inputs(seed: int = 0) -> dict:
    keys = jax.random.split(jax.random.key(seed), 7)
    return {
        "queries": draw_queries(jax.random.fold_in(keys[6], 71), 0),
        "key_states": draw_key_states(jax.random.fold_in(keys[6], 71), 0),
        "value_states": noise(keys[2], (SECTIONS, TOKENS, HEADS * DH), 1.0, 6.0, ((0, 4), (1, 8))),
        "upstream": noise(keys[3], (SECTIONS, TOKENS, HEADS * DH), 1.0, 6.0, ((0, 4), (1, 8))),
        "layout": draw_layout(jax.random.fold_in(keys[6], 71), 0),
        "segments": jax.vmap(lambda own: jnp.searchsorted(jnp.cumsum(uneven(own, NB // 4 + 1, NB, NB // 2, 0)), jnp.arange(NB), side="right"))(jax.random.split(keys[5], SECTIONS)).reshape((SECTIONS, NB)).astype(jnp.int32),
    }


def gather_blocks(blocks, layout):
    head_index = jnp.arange(layout.shape[0])[:, None, None]
    picked = blocks[layout, :, head_index, :]
    return picked.reshape(layout.shape[0], layout.shape[1], layout.shape[2] * blocks.shape[1], blocks.shape[3])

def visible_mask(layout, segments, block_rows):
    block_count = layout.shape[1]
    query_block = jnp.arange(block_count)[None, :, None]
    same_doc = segments[layout] == segments[query_block]
    earlier = layout < query_block
    position = jnp.arange(block_rows)
    within = position[None, None, None, None, :] <= position[None, None, :, None, None]
    diagonal = (layout == query_block)[:, :, None, :, None] & within
    visible = same_doc[:, :, None, :, None] & (earlier[:, :, None, :, None] | diagonal)
    return visible.reshape(layout.shape[0], block_count, block_rows, layout.shape[2] * block_rows)

def scatter_blocks(picked, layout, block_rows):
    head_count, block_count, slot_count = layout.shape
    head_dim = picked.shape[-1]
    pieces = picked.reshape(head_count, block_count, slot_count, block_rows * head_dim)
    onehot = (layout[..., None] == jnp.arange(block_count)).astype(jnp.float32)
    summed = jnp.einsum('hasb,hase->hbe', onehot, pieces, precision=lax.Precision.HIGHEST)
    return summed.reshape(head_count, block_count, block_rows, head_dim).transpose(1, 2, 0, 3)

def section_pass(inputs):
    queries, key_states, value_states, grad_out, layout, segments = inputs
    block_shape = (NB, BLK, HEADS, DH)
    score_scale = 1.0 / math.sqrt(DH)
    query_blocks = queries.reshape(block_shape).astype(jnp.float32)
    key_rows = gather_blocks(key_states.reshape(block_shape), layout).astype(jnp.float32)
    value_rows = gather_blocks(value_states.reshape(block_shape), layout).astype(jnp.float32)
    visible = visible_mask(layout, segments, BLK)
    scores = jnp.einsum('aihd,hamd->haim', query_blocks, key_rows) * score_scale
    scores = jnp.where(visible, scores, -jnp.inf)
    row_max = lax.optimization_barrier(jnp.max(scores, axis=-1, keepdims=True))
    raised = jnp.exp(scores - row_max)
    weights = raised / lax.optimization_barrier(jnp.sum(raised, axis=-1, keepdims=True))
    weights_low = lax.optimization_barrier(weights.astype(jnp.bfloat16)).astype(jnp.float32)
    attended = jnp.einsum('haim,hamd->aihd', weights_low, value_rows).astype(jnp.bfloat16)
    attended_wide = lax.optimization_barrier(attended).astype(jnp.float32)
    grad_blocks = grad_out.reshape(block_shape).astype(jnp.float32)
    grad_weight = jnp.einsum('aihd,hamd->haim', grad_blocks, value_rows)
    row_inner = lax.optimization_barrier(jnp.sum(grad_blocks * attended_wide, axis=-1)).transpose(2, 0, 1)[..., None]
    grad_score = (weights * (grad_weight - row_inner)).astype(jnp.bfloat16)
    grad_score = lax.optimization_barrier(grad_score).astype(jnp.float32)
    grad_query = (jnp.einsum('haim,hamd->aihd', grad_score, key_rows) * score_scale).astype(jnp.bfloat16)
    grad_key_rows = jnp.einsum('haim,aihd->hamd', grad_score, query_blocks) * score_scale
    grad_value_rows = jnp.einsum('haim,aihd->hamd', weights_low, grad_blocks)
    grad_key = scatter_blocks(grad_key_rows, layout, BLK).astype(jnp.bfloat16)
    grad_value = scatter_blocks(grad_value_rows, layout, BLK).astype(jnp.bfloat16)
    flat_shape = (TOKENS, HEADS * DH)
    return (attended.reshape(flat_shape), grad_query.reshape(flat_shape), grad_key.reshape(flat_shape), grad_value.reshape(flat_shape))

def reference(queries, key_states, value_states, upstream, layout, segments):
    grad_all = jnp.roll(upstream, -1, axis=0)
    results = lax.map(section_pass, (queries, key_states, value_states, grad_all, layout, segments))
    return (results[0], results[1], results[2], results[3])
```

```python
import functools
import math

import jax
import jax.numpy as jnp
from jax import lax
from jax.experimental import pallas as pl
from jax.experimental.pallas import tpu as pltpu
from jax.sharding import PartitionSpec as P

HEADS = 16
BLK = 128
CORES = 2
LEAD = 2
HIDDEN = -1e30
MESH = pl.DeviceIdType.MESH


def dot(left, right, left_dim, right_dim):
    return lax.dot_general(
        left, right, (((left_dim,), (right_dim,)), ((), ())), preferred_element_type=jnp.float32
    )


def kernel(
    sections,
    count,
    head_dim,
    seg_ref,
    far_ref,
    q_ref,
    k_ref,
    v_ref,
    u_ref,
    o_ref,
    dq_ref,
    dk_ref,
    dv_ref,
    kvw,
    qb,
    gb,
    fart,
    bias,
    acc,
    snd,
    rcv,
    st,
    up_send,
    up_recv,
    fw_send,
    fw_recv,
    dn_send,
    dn_recv,
    xc_send,
    xc_recv,
    u_send,
    u_recv,
    fa_send,
    fa_recv,
    ou_send,
    ou_recv,
):
    chips = count // CORES
    heads = HEADS // CORES
    reach = count // 2 - 1
    hops = (reach + 1) // 2
    scale = 1.0 / math.sqrt(head_dim)
    sec = lax.axis_index("section")
    me = lax.axis_index("ctx")
    chip = me // CORES
    core = me % CORES
    other = 1 - core
    sibling = chip * CORES + other
    before_sec = (sec + sections - 1) % sections
    after_sec = (sec + 1) % sections
    inputs = (q_ref, k_ref, v_ref)
    results = (o_ref, dq_ref, dk_ref, dv_ref)

    def cols(h):
        return pl.ds(pl.multiple_of(h * head_dim, head_dim), head_dim)

    def half(side):
        return pl.ds(pl.multiple_of(side * (heads * head_dim), heads * head_dim), heads * head_dim)

    def rows(block, n=1):
        if isinstance(block, int):
            return pl.ds(block * BLK, n * BLK)
        return pl.ds(pl.multiple_of(block * BLK, BLK), n * BLK)

    def hop_rows(hop):
        first = reach - 2 * hop
        return rows(0, 1) if first < 0 else rows(first, 2)

    def remote(src, dst, send, recv, section, ctx):
        return pltpu.make_async_remote_copy(
            src_ref=src,
            dst_ref=dst,
            send_sem=send,
            recv_sem=recv,
            device_id=(section, ctx),
            device_id_type=MESH,
        )

    def up(h, to_core, kv, source):
        return remote(
            inputs[1 + kv].at[0, :, cols(to_core * heads + h)],
            kvw.at[kv, rows(reach - 2 + source), cols(h)],
            up_send.at[to_core, kv, h],
            up_recv.at[source, kv, h],
            sec,
            me - core + CORES + to_core,
        )

    def forward(h, hop):
        full = reach - 2 * hop >= 0
        source = rows(reach - 2 * hop + 2, 2) if full else rows(reach - 2 * hop + 3, 1)
        return remote(
            kvw.at[:, source, cols(h)],
            kvw.at[:, hop_rows(hop), cols(h)],
            fw_send.at[hop - 2, h],
            fw_recv.at[hop - 2, h],
            sec,
            me + CORES,
        )

    def down(h, hop):
        return remote(
            snd.at[:, hop_rows(hop), cols(h)],
            rcv.at[:, hop_rows(hop), cols(h)],
            dn_send.at[hop - 1, h],
            dn_recv.at[hop - 1, h],
            sec,
            me - CORES,
        )

    def swap(x, block):
        dst = qb.at[rows(block), :] if x == 0 else kvw.at[x - 1, rows(reach + block), :]
        return remote(
            inputs[x].at[0, :, half(other)], dst, xc_send.at[x], xc_recv.at[x], sec, sibling
        )

    def relay(h, to_core, source):
        return remote(
            u_ref.at[0, :, cols(to_core * heads + h)],
            gb.at[rows(source), cols(h)],
            u_send.at[to_core, h],
            u_recv.at[source, h],
            before_sec,
            me - core + to_core,
        )

    held = HEADS // count
    side = me // chips
    place = me % chips

    def spread(to_chip, slot):
        return remote(
            far_ref,
            fart.at[pl.ds(slot * held, held)],
            fa_send.at[to_chip],
            fa_recv.at[slot],
            sec,
            to_chip * CORES + side,
        )

    def give(h, x):
        return remote(
            st.at[x, rows(other), cols(h)],
            results[x].at[0, :, cols(core * heads + h)],
            ou_send.at[x, h],
            ou_recv.at[x, h],
            sec,
            sibling,
        )

    def take(h, x):
        return remote(
            st.at[x, rows(core), cols(h)],
            results[x].at[0, :, cols(other * heads + h)],
            ou_send.at[x, h],
            ou_recv.at[x, h],
            sec,
            sibling,
        )

    barrier = pltpu.get_barrier_semaphore()
    for step in range(1, count):
        pl.semaphore_signal(
            barrier, inc=1, device_id=(sec, (me + step) % count), device_id_type=MESH
        )
    for section in (before_sec, after_sec):
        for to_core in range(CORES):
            pl.semaphore_signal(
                barrier, inc=1, device_id=(section, me - core + to_core), device_id_type=MESH
            )

    for hop in range(1, hops + 1):

        @pl.when(chip < hop)
        def _():
            first = max(reach - 2 * hop, 0)
            height = (1 if reach - 2 * hop < 0 else 2) * BLK
            kvw[:, pl.ds(first * BLK, height), :] = jnp.zeros(
                (2, height, heads * head_dim), kvw.dtype
            )

    qb[rows(core), :] = q_ref[0, :, half(core)]
    kvw[0, rows(reach + core), :] = k_ref[0, :, half(core)]
    kvw[1, rows(reach + core), :] = v_ref[0, :, half(core)]

    pl.semaphore_wait(barrier, count - 1 + 2 * CORES)

    def send_up(h):
        @pl.when(chip < chips - 1)
        def _():
            for kv in range(2):
                for to_core in range(CORES):
                    up(h, to_core, kv, core).start()

    def send_relay(h):
        for to_core in range(CORES):
            relay(h, to_core, core).start()

    for h in range(LEAD):
        send_up(h)
    for step in range(chips):

        @pl.when(jnp.logical_not(step * CORES + side == me))
        def _():
            spread(step, place).start()

    @pl.when(side == core)
    def _():
        fart[pl.ds(place * held, held)] = far_ref[...]

    for x in range(3):
        swap(x, core).start()
    for h in range(LEAD + 1):
        send_relay(h)

    row_id = lax.broadcasted_iota(jnp.int32, (BLK, BLK), 0)
    col_id = lax.broadcasted_iota(jnp.int32, (BLK, BLK), 1)
    causal = jnp.where(col_id <= row_id, 0.0, HIDDEN).astype(jnp.float32)
    for qi in range(2):
        doc = seg_ref[0, chip * CORES + qi]
        for i in range(reach + 1):
            block = chip * CORES + qi - reach + i
            same = jnp.logical_and(block >= 0, seg_ref[0, jnp.maximum(block, 0)] == doc)
            shown = jnp.where(same, 0.0, HIDDEN).astype(jnp.float32)
            here = causal if i == reach else jnp.zeros((BLK, BLK), jnp.float32)
            bias[pl.ds(qi * BLK, BLK), pl.ds(i * BLK, BLK)] = here + shown

    for x in range(3):
        swap(x, other).wait_recv()
    for step in range(chips):

        @pl.when(jnp.logical_not(core * chips + step == me))
        def _():
            spread(0, step).wait_recv()

    def compute(h):
        part = cols(h)
        weights_of, score_of, q_of, g_of = [], [], [], []
        for qi in range(2):
            q = qb[pl.ds(qi * BLK, BLK), part]
            g = gb[pl.ds(qi * BLK, BLK), part]
            keys = kvw[0, pl.ds(qi * BLK, (reach + 1) * BLK), part]
            values = kvw[1, pl.ds(qi * BLK, (reach + 1) * BLK), part]
            block = chip * CORES + qi
            far = fart[h, pl.ds(block, 1), :]
            pieces = []
            for i in range(reach + 1):
                if reach - i >= 3:
                    pieces.append(
                        jnp.where(far == block - reach + i, 0.0, HIDDEN).astype(jnp.float32)
                    )
                else:
                    pieces.append(jnp.zeros((1, BLK), jnp.float32))
            scores = dot(q, keys, 1, 1) * scale + bias[pl.ds(qi * BLK, BLK), :]
            scores = scores + jnp.concatenate(pieces, axis=1)
            row_max = jnp.max(scores, axis=-1, keepdims=True)
            raised = jnp.exp(scores - row_max)
            weights = raised * (1.0 / jnp.sum(raised, axis=-1, keepdims=True))
            low = weights.astype(jnp.bfloat16)
            attended = dot(low, values, 1, 0).astype(jnp.bfloat16)
            st[0, pl.ds(qi * BLK, BLK), part] = attended
            inner = jnp.sum(
                g.astype(jnp.float32) * attended.astype(jnp.float32), axis=-1, keepdims=True
            )
            score = (weights * (dot(g, values, 1, 1) - inner)).astype(jnp.bfloat16)
            st[1, pl.ds(qi * BLK, BLK), part] = (dot(score, keys, 1, 0) * scale).astype(
                jnp.bfloat16
            )
            weights_of.append(low)
            score_of.append(score)
            q_of.append(q)
            g_of.append(g)
        for kv, (left, right, factor) in enumerate(
            ((score_of, q_of, scale), (weights_of, g_of, 1.0))
        ):
            acc[h, kv, pl.ds(0, BLK), :] = dot(left[0][:, :BLK], right[0], 0, 0) * factor
            acc[h, kv, pl.ds((reach + 1) * BLK, BLK), :] = (
                dot(left[1][:, reach * BLK :], right[1], 0, 0) * factor
            )
            both = jnp.concatenate([left[0][:, BLK:], left[1][:, : reach * BLK]], axis=0)
            acc[h, kv, pl.ds(BLK, reach * BLK), :] = (
                dot(both, jnp.concatenate(right, axis=0), 0, 0) * factor
            )

    def hand_out(h, x):
        give(h, x).start()
        results[x][0, :, cols(core * heads + h)] = st[x, rows(core), cols(h)]

    def send_down(h, hop):
        @pl.when(chip >= hop)
        def _():
            for kv in range(2):
                snd[kv, hop_rows(hop), cols(h)] = acc[h, kv, hop_rows(hop), :].astype(jnp.bfloat16)
            down(h, hop).start()

    def at(h, action):
        @pl.when(jnp.logical_and(h >= 0, h < heads))
        def _():
            action(h)

    def arrive(hop):
        def action(h):
            @pl.when(chip >= hop)
            def _():
                if hop == 1:
                    for source in range(CORES):
                        for kv in range(2):
                            up(h, 0, kv, source).wait_recv()
                else:
                    forward(h, hop).wait_recv()

            if hop < hops:

                @pl.when(jnp.logical_and(chip >= hop, chip < chips - 1))
                def _():
                    forward(h, hop + 1).start()

        return action

    def work(h):
        for source in range(CORES):
            relay(h, 0, source).wait_recv()
        compute(h)
        send_down(h, hops)
        for x in range(2):
            hand_out(h, x)

    def settle(hop):
        def action(h):
            target = max(reach - 2 * hop + 2, 0) if reach - 2 * hop >= 0 else 2
            if reach - 2 * hop < 0:
                target = reach - 2 * hop + 3
            height = BLK if reach - 2 * hop < 0 else 2 * BLK

            @pl.when(jnp.logical_and(chip < chips - 1, chip + 1 >= hop))
            def _():
                down(h, hop).wait_recv()
                for kv in range(2):
                    acc[h, kv, pl.ds(target * BLK, height), :] += rcv[
                        kv, hop_rows(hop), cols(h)
                    ].astype(jnp.float32)

            if hop > 1:
                send_down(h, hop - 1)
            else:
                for kv in range(2):
                    st[2 + kv, :, cols(h)] = acc[h, kv, pl.ds(reach * BLK, 2 * BLK), :].astype(
                        jnp.bfloat16
                    )
                    hand_out(h, 2 + kv)

        return action

    @pl.loop(0, heads + 2 * hops - 1)
    def _(i):
        @pl.when(i + LEAD < heads)
        def _():
            send_up(i + LEAD)

        @pl.when(i + LEAD + 1 < heads)
        def _():
            send_relay(i + LEAD + 1)

        for hop in range(1, hops + 1):
            at(i - (hop - 1), arrive(hop))
        at(i - (hops - 1), work)
        for hop in range(hops, 0, -1):
            at(i - (hops - 1) - 1 - (hops - hop), settle(hop))

    for x in range(3):
        swap(x, core).wait_send()
    for step in range(chips):

        @pl.when(jnp.logical_not(step * CORES + side == me))
        def _():
            spread(step, place).wait_send()

    @pl.loop(0, heads)
    def _(h):
        @pl.when(chip < chips - 1)
        def _():
            for kv in range(2):
                for to_core in range(CORES):
                    up(h, to_core, kv, core).wait_send()

        for hop in range(2, hops + 1):

            @pl.when(jnp.logical_and(chip >= hop - 1, chip < chips - 1))
            def _():
                forward(h, hop).wait_send()

        for hop in range(1, hops + 1):

            @pl.when(chip >= hop)
            def _():
                down(h, hop).wait_send()

        for to_core in range(CORES):
            relay(h, to_core, core).wait_send()
        for x in range(4):
            give(h, x).wait_send()
            take(h, x).wait_recv()


def local(queries, key_states, value_states, upstream, layout, segments):
    sections = lax.axis_size("section")
    count = lax.axis_size("ctx")
    width = queries.shape[-1]
    head_dim = width // HEADS
    heads = HEADS // CORES
    held, blocks, _ = layout.shape[1:]
    chips = count // CORES
    reach = count // 2 - 1
    hops = (reach + 1) // 2
    plan = layout[0]
    distance = (jnp.arange(blocks, dtype=jnp.int32)[None, :, None] - plan + blocks) % blocks
    far = jnp.sum(jnp.where(distance >= 3, plan, 0), axis=-1)
    far = jnp.broadcast_to(far[:, :, None], (held, blocks, BLK)).astype(jnp.int32)
    vmem = pl.BlockSpec(memory_space=pltpu.VMEM)
    part = heads * head_dim
    dma = pltpu.SemaphoreType.DMA
    return tuple(
        pl.pallas_call(
            functools.partial(kernel, sections, count, head_dim),
            out_shape=[jax.ShapeDtypeStruct(queries.shape, jnp.bfloat16)] * 4,
            in_specs=[pl.BlockSpec(memory_space=pltpu.SMEM)] + [vmem] * 5,
            out_specs=[vmem] * 4,
            scratch_shapes=[
                pltpu.VMEM((2, (reach + 2) * BLK, part), jnp.bfloat16),
                pltpu.VMEM((2 * BLK, part), jnp.bfloat16),
                pltpu.VMEM((2 * BLK, part), jnp.bfloat16),
                pltpu.VMEM((heads, blocks, BLK), jnp.int32),
                pltpu.VMEM((2 * BLK, (reach + 1) * BLK), jnp.float32),
                pltpu.VMEM((heads, 2, (reach + 2) * BLK, head_dim), jnp.float32),
                pltpu.VMEM((2, reach * BLK, part), jnp.bfloat16),
                pltpu.VMEM((2, reach * BLK, part), jnp.bfloat16),
                pltpu.VMEM((4, 2 * BLK, part), jnp.bfloat16),
                dma((CORES, 2, heads)),
                dma((CORES, 2, heads)),
                dma((max(hops - 1, 1), heads)),
                dma((max(hops - 1, 1), heads)),
                dma((hops, heads)),
                dma((hops, heads)),
                dma((3,)),
                dma((3,)),
                dma((CORES, heads)),
                dma((CORES, heads)),
                dma((chips,)),
                dma((chips,)),
                dma((4, heads)),
                dma((4, heads)),
            ],
            compiler_params=pltpu.CompilerParams(
                collective_id=0, has_side_effects=True, vmem_limit_bytes=44 * 1024 * 1024
            ),
        )(segments, far, queries, key_states, value_states, upstream)
    )


def solution(mesh):
    field = P("section", "ctx", None)
    return jax.shard_map(
        local,
        mesh=mesh,
        in_specs=(field,) * 4 + (P("section", "ctx", None, None), P("section", None)),
        out_specs=(field,) * 4,
        check_vma=False,
    )
```

```python
import functools
import math

import jax
import jax.numpy as jnp
from jax import lax
from jax.experimental import pallas as pl
from jax.experimental.pallas import tpu as pltpu
from jax.sharding import PartitionSpec as P

HEADS = 16
BLK = 128
CORES = 2
LEAD = 1
HIDDEN = -1e30
MESH = pl.DeviceIdType.MESH


def dot(left, right, left_dim, right_dim):
    return lax.dot_general(
        left, right, (((left_dim,), (right_dim,)), ((), ())), preferred_element_type=jnp.float32
    )


def kernel(
    sections,
    count,
    head_dim,
    seg_ref,
    far_ref,
    q_ref,
    k_ref,
    v_ref,
    u_ref,
    o_ref,
    dq_ref,
    dk_ref,
    dv_ref,
    kvw,
    qb,
    gb,
    fart,
    bias,
    acc,
    snd,
    rcv,
    st,
    up_send,
    up_recv,
    fw_send,
    fw_recv,
    dn_send,
    dn_recv,
    xc_send,
    xc_recv,
    u_send,
    u_recv,
    fa_send,
    fa_recv,
    ou_send,
    ou_recv,
    lo_sem,
):
    chips = count // CORES
    heads = HEADS // CORES
    reach = count // 2 - 1
    hops = (reach + 1) // 2
    scale = 1.0 / math.sqrt(head_dim)
    sec = lax.axis_index("section")
    me = lax.axis_index("ctx")
    chip = me // CORES
    core = me % CORES
    other = 1 - core
    sibling = chip * CORES + other
    before_sec = (sec + sections - 1) % sections
    after_sec = (sec + 1) % sections
    inputs = (q_ref, k_ref, v_ref)
    results = (o_ref, dq_ref, dk_ref, dv_ref)

    def cols(h):
        return pl.ds(pl.multiple_of(h * head_dim, head_dim), head_dim)

    def half(side):
        return pl.ds(pl.multiple_of(side * (heads * head_dim), heads * head_dim), heads * head_dim)

    def rows(block, n=1):
        if isinstance(block, int):
            return pl.ds(block * BLK, n * BLK)
        return pl.ds(pl.multiple_of(block * BLK, BLK), n * BLK)

    def hop_rows(hop):
        first = reach - 2 * hop
        return rows(0, 1) if first < 0 else rows(first, 2)

    def remote(src, dst, send, recv, section, ctx):
        return pltpu.make_async_remote_copy(
            src_ref=src,
            dst_ref=dst,
            send_sem=send,
            recv_sem=recv,
            device_id=(section, ctx),
            device_id_type=MESH,
        )

    def up(h, to_core, kv, source):
        return remote(
            inputs[1 + kv].at[0, :, cols(to_core * heads + h)],
            kvw.at[kv, rows(reach - 2 + source), cols(h)],
            up_send.at[to_core, kv, h],
            up_recv.at[source, kv, h],
            sec,
            me - core + CORES + to_core,
        )

    def forward(h, hop):
        full = reach - 2 * hop >= 0
        source = rows(reach - 2 * hop + 2, 2) if full else rows(reach - 2 * hop + 3, 1)
        return remote(
            kvw.at[:, source, cols(h)],
            kvw.at[:, hop_rows(hop), cols(h)],
            fw_send.at[hop - 2, h],
            fw_recv.at[hop - 2, h],
            sec,
            me + CORES,
        )

    def down_rows(hop):
        if hop > hops:
            return rows(1, 1)
        return rows(2, 1) if hop == hops - 1 else hop_rows(hop)

    def down(h, hop):
        return remote(
            snd.at[:, down_rows(hop), cols(h)],
            rcv.at[:, down_rows(hop), cols(h)],
            dn_send.at[hop - 1, h],
            dn_recv.at[hop - 1, h],
            sec,
            me - CORES,
        )

    def swap(x, block):
        dst = qb.at[rows(block), :] if x == 0 else kvw.at[x - 1, rows(reach + block), :]
        return remote(
            inputs[x].at[0, :, half(other)], dst, xc_send.at[x], xc_recv.at[x], sec, sibling
        )

    def relay(h, to_core, source):
        return remote(
            u_ref.at[0, :, cols(to_core * heads + h)],
            gb.at[rows(source), cols(h)],
            u_send.at[to_core, h],
            u_recv.at[source, h],
            before_sec,
            me - core + to_core,
        )

    held = HEADS // count
    side = me // chips
    place = me % chips

    def spread(to_chip, slot):
        return remote(
            far_ref,
            fart.at[pl.ds(slot * held, held)],
            fa_send.at[to_chip],
            fa_recv.at[slot],
            sec,
            to_chip * CORES + side,
        )

    def give(h, x):
        return remote(
            st.at[x, rows(other), cols(h)],
            results[x].at[0, :, cols(core * heads + h)],
            ou_send.at[x, h],
            ou_recv.at[x, h],
            sec,
            sibling,
        )

    def take(h, x):
        return remote(
            st.at[x, rows(core), cols(h)],
            results[x].at[0, :, cols(other * heads + h)],
            ou_send.at[x, h],
            ou_recv.at[x, h],
            sec,
            sibling,
        )

    def own(x):
        dst = qb.at[rows(core), :] if x == 0 else kvw.at[x - 1, rows(reach + core), :]
        return pltpu.make_async_copy(inputs[x].at[0, :, half(core)], dst, lo_sem.at[x])

    def own_far():
        return pltpu.make_async_copy(far_ref, fart.at[pl.ds(place * held, held)], lo_sem.at[3])

    barrier = pltpu.get_barrier_semaphore()
    for step in range(1, count):
        pl.semaphore_signal(
            barrier, inc=1, device_id=(sec, (me + step) % count), device_id_type=MESH
        )
    for section in (before_sec, after_sec):
        for to_core in range(CORES):
            pl.semaphore_signal(
                barrier, inc=1, device_id=(section, me - core + to_core), device_id_type=MESH
            )

    for hop in range(1, hops + 1):

        @pl.when(chip < hop)
        def _():
            first = max(reach - 2 * hop, 0)
            height = (1 if reach - 2 * hop < 0 else 2) * BLK
            kvw[:, pl.ds(first * BLK, height), :] = jnp.zeros(
                (2, height, heads * head_dim), kvw.dtype
            )

    for x in range(3):
        own(x).start()

    @pl.when(side == core)
    def _():
        own_far().start()

    pl.semaphore_wait(barrier, count - 1 + 2 * CORES)

    def send_up(h):
        @pl.when(chip < chips - 1)
        def _():
            for kv in range(2):
                for to_core in range(CORES):
                    up(h, to_core, kv, core).start()

    def send_relay(h):
        for to_core in range(CORES):
            relay(h, to_core, core).start()

    for h in range(LEAD):
        send_up(h)
    for step in range(chips):

        @pl.when(jnp.logical_not(step * CORES + side == me))
        def _():
            spread(step, place).start()

    for x in range(3):
        swap(x, core).start()
    for h in range(LEAD + 1):
        send_relay(h)

    row_id = lax.broadcasted_iota(jnp.int32, (BLK, BLK), 0)
    col_id = lax.broadcasted_iota(jnp.int32, (BLK, BLK), 1)
    causal = jnp.where(col_id <= row_id, 0.0, HIDDEN).astype(jnp.float32)
    for qi in range(2):
        doc = seg_ref[0, chip * CORES + qi]
        for i in range(reach + 1):
            block = chip * CORES + qi - reach + i
            same = jnp.logical_and(block >= 0, seg_ref[0, jnp.maximum(block, 0)] == doc)
            shown = jnp.where(same, 0.0, HIDDEN).astype(jnp.float32)
            here = causal if i == reach else jnp.zeros((BLK, BLK), jnp.float32)
            bias[pl.ds(qi * BLK, BLK), pl.ds(i * BLK, BLK)] = here + shown

    for x in range(3):
        own(x).wait()
        swap(x, other).wait_recv()

    @pl.when(side == core)
    def _():
        own_far().wait()

    for step in range(chips):

        @pl.when(jnp.logical_not(core * chips + step == me))
        def _():
            spread(0, step).wait_recv()

    def compute(h):
        part = cols(h)
        weights_of, score_of, q_of, g_of = [], [], [], []
        for qi in range(2):
            q = qb[pl.ds(qi * BLK, BLK), part]
            g = gb[pl.ds(qi * BLK, BLK), part]
            keys = kvw[0, pl.ds(qi * BLK, (reach + 1) * BLK), part]
            values = kvw[1, pl.ds(qi * BLK, (reach + 1) * BLK), part]
            block = chip * CORES + qi
            far = fart[h, pl.ds(block, 1), :]
            pieces = []
            for i in range(reach + 1):
                if reach - i >= 3:
                    pieces.append(
                        jnp.where(far == block - reach + i, 0.0, HIDDEN).astype(jnp.float32)
                    )
                else:
                    pieces.append(jnp.zeros((1, BLK), jnp.float32))
            scores = dot(q, keys, 1, 1) * scale + bias[pl.ds(qi * BLK, BLK), :]
            scores = scores + jnp.concatenate(pieces, axis=1)
            row_max = jnp.max(scores, axis=-1, keepdims=True)
            raised = jnp.exp(scores - row_max)
            weights = raised * (1.0 / jnp.sum(raised, axis=-1, keepdims=True))
            low = weights.astype(jnp.bfloat16)
            attended = dot(low, values, 1, 0).astype(jnp.bfloat16)
            st[0, pl.ds(qi * BLK, BLK), part] = attended
            inner = jnp.sum(
                g.astype(jnp.float32) * attended.astype(jnp.float32), axis=-1, keepdims=True
            )
            score = (weights * (dot(g, values, 1, 1) - inner)).astype(jnp.bfloat16)
            st[1, pl.ds(qi * BLK, BLK), part] = (dot(score, keys, 1, 0) * scale).astype(
                jnp.bfloat16
            )
            weights_of.append(low)
            score_of.append(score)
            q_of.append(q)
            g_of.append(g)
        for kv, (left, right, factor) in enumerate(
            ((score_of, q_of, scale), (weights_of, g_of, 1.0))
        ):
            acc[h, kv, pl.ds(0, BLK), :] = dot(left[0][:, :BLK], right[0], 0, 0) * factor
            acc[h, kv, pl.ds((reach + 1) * BLK, BLK), :] = (
                dot(left[1][:, reach * BLK :], right[1], 0, 0) * factor
            )
            both = jnp.concatenate([left[0][:, BLK:], left[1][:, : reach * BLK]], axis=0)
            acc[h, kv, pl.ds(BLK, reach * BLK), :] = (
                dot(both, jnp.concatenate(right, axis=0), 0, 0) * factor
            )

    def hand_out(h, x):
        give(h, x).start()
        results[x][0, :, cols(core * heads + h)] = st[x, rows(core), cols(h)]

    def send_down(h, hop):
        @pl.when(chip >= (hops - 1 if hop > hops else hop))
        def _():
            for kv in range(2):
                snd[kv, down_rows(hop), cols(h)] = acc[h, kv, down_rows(hop), :].astype(
                    jnp.bfloat16
                )
            down(h, hop).start()

    def at(h, action):
        @pl.when(jnp.logical_and(h >= 0, h < heads))
        def _():
            action(h)

    def arrive(hop):
        def action(h):
            @pl.when(chip >= hop)
            def _():
                if hop == 1:
                    for source in range(CORES):
                        for kv in range(2):
                            up(h, 0, kv, source).wait_recv()
                else:
                    forward(h, hop).wait_recv()

            if hop < hops:

                @pl.when(jnp.logical_and(chip >= hop, chip < chips - 1))
                def _():
                    forward(h, hop + 1).start()

        return action

    def work(h):
        for source in range(CORES):
            relay(h, 0, source).wait_recv()
        compute(h)
        send_down(h, hops)
        if hops > 1:
            send_down(h, hops + 1)
        for x in range(2):
            hand_out(h, x)

    def settle(hop):
        def action(h):
            target = max(reach - 2 * hop + 2, 0) if reach - 2 * hop >= 0 else 2
            if reach - 2 * hop < 0:
                target = reach - 2 * hop + 3
            height = BLK if reach - 2 * hop < 0 else 2 * BLK

            @pl.when(jnp.logical_and(chip < chips - 1, chip + 1 >= hop))
            def _():
                down(h, hop).wait_recv()
                if hop == hops - 1:
                    down(h, hops + 1).wait_recv()
                for kv in range(2):
                    acc[h, kv, pl.ds(target * BLK, height), :] += rcv[
                        kv, hop_rows(hop), cols(h)
                    ].astype(jnp.float32)

            if hop > 1:
                send_down(h, hop - 1)
            else:
                for kv in range(2):
                    st[2 + kv, :, cols(h)] = acc[h, kv, pl.ds(reach * BLK, 2 * BLK), :].astype(
                        jnp.bfloat16
                    )
                    hand_out(h, 2 + kv)

        return action

    @pl.loop(0, heads + 2 * hops - 1)
    def _(i):
        @pl.when(i + LEAD < heads)
        def _():
            send_up(i + LEAD)

        @pl.when(i + LEAD + 1 < heads)
        def _():
            send_relay(i + LEAD + 1)

        for hop in range(1, hops):
            at(i - (hop - 1), arrive(hop))
        for hop in range(hops, 0, -1):
            at(i - (hops - 1) - 1 - (hops - hop), settle(hop))
        at(i - (hops - 1), arrive(hops))
        at(i - (hops - 1), work)

    for x in range(3):
        swap(x, core).wait_send()
    for step in range(chips):

        @pl.when(jnp.logical_not(step * CORES + side == me))
        def _():
            spread(step, place).wait_send()

    @pl.loop(0, heads)
    def _(h):
        @pl.when(chip < chips - 1)
        def _():
            for kv in range(2):
                for to_core in range(CORES):
                    up(h, to_core, kv, core).wait_send()

        for hop in range(2, hops + 1):

            @pl.when(jnp.logical_and(chip >= hop - 1, chip < chips - 1))
            def _():
                forward(h, hop).wait_send()

        for hop in range(1, hops + 1):

            @pl.when(chip >= hop)
            def _():
                down(h, hop).wait_send()
                if hop == hops - 1:
                    down(h, hops + 1).wait_send()

        for to_core in range(CORES):
            relay(h, to_core, core).wait_send()
        for x in range(4):
            give(h, x).wait_send()
            take(h, x).wait_recv()


def store(*refs):
    sems = refs[8]
    copies = [pltpu.make_async_copy(refs[x], refs[4 + x], sems.at[x]) for x in range(4)]
    for copy in copies:
        copy.start()
    for copy in copies:
        copy.wait()


def local(queries, key_states, value_states, upstream, layout, segments):
    sections = lax.axis_size("section")
    count = lax.axis_size("ctx")
    width = queries.shape[-1]
    head_dim = width // HEADS
    heads = HEADS // CORES
    held, blocks, _ = layout.shape[1:]
    chips = count // CORES
    reach = count // 2 - 1
    hops = (reach + 1) // 2
    plan = layout[0]
    distance = (jnp.arange(blocks, dtype=jnp.int32)[None, :, None] - plan + blocks) % blocks
    far = jnp.sum(jnp.where(distance >= 3, plan, 0), axis=-1)
    far = jnp.broadcast_to(far[:, :, None], (held, blocks, BLK)).astype(jnp.int32)
    away = pl.BlockSpec(memory_space=pl.ANY)
    vmem = pl.BlockSpec(memory_space=pltpu.VMEM)
    part = heads * head_dim
    dma = pltpu.SemaphoreType.DMA
    shapes = [jax.ShapeDtypeStruct(queries.shape, jnp.bfloat16)] * 4
    made = tuple(
        pl.pallas_call(
            functools.partial(kernel, sections, count, head_dim),
            out_shape=shapes,
            in_specs=[pl.BlockSpec(memory_space=pltpu.SMEM)] + [away] * 5,
            out_specs=[vmem] * 4,
            scratch_shapes=[
                pltpu.VMEM((2, (reach + 2) * BLK, part), jnp.bfloat16),
                pltpu.VMEM((2 * BLK, part), jnp.bfloat16),
                pltpu.VMEM((2 * BLK, part), jnp.bfloat16),
                pltpu.VMEM((heads, blocks, BLK), jnp.int32),
                pltpu.VMEM((2 * BLK, (reach + 1) * BLK), jnp.float32),
                pltpu.VMEM((heads, 2, (reach + 2) * BLK, head_dim), jnp.float32),
                pltpu.VMEM((2, reach * BLK, part), jnp.bfloat16),
                pltpu.VMEM((2, reach * BLK, part), jnp.bfloat16),
                pltpu.VMEM((4, 2 * BLK, part), jnp.bfloat16),
                dma((CORES, 2, heads)),
                dma((CORES, 2, heads)),
                dma((max(hops - 1, 1), heads)),
                dma((max(hops - 1, 1), heads)),
                dma((hops + 1, heads)),
                dma((hops + 1, heads)),
                dma((3,)),
                dma((3,)),
                dma((CORES, heads)),
                dma((CORES, heads)),
                dma((chips,)),
                dma((chips,)),
                dma((4, heads)),
                dma((4, heads)),
                dma((4,)),
            ],
            compiler_params=pltpu.CompilerParams(
                collective_id=0, has_side_effects=True, vmem_limit_bytes=56 * 1024 * 1024
            ),
        )(segments, far, queries, key_states, value_states, upstream)
    )
    return tuple(
        pl.pallas_call(
            store,
            out_shape=shapes,
            in_specs=[vmem] * 4,
            out_specs=[away] * 4,
            scratch_shapes=[dma((4,))],
        )(*made)
    )


def solution(mesh):
    field = P("section", "ctx", None)
    return jax.shard_map(
        local,
        mesh=mesh,
        in_specs=(field,) * 4 + (P("section", "ctx", None, None), P("section", None)),
        out_specs=(field,) * 4,
        check_vma=False,
    )
```

```python
import functools
import math

import jax
import jax.numpy as jnp
from jax import lax
from jax.experimental import pallas as pl
from jax.experimental.pallas import tpu as pltpu
from jax.sharding import PartitionSpec as P

HEADS = 16
BLK = 128
CORES = 2
LEAD = 1
HIDDEN = -1e30
MESH = pl.DeviceIdType.MESH


def dot(left, right, left_dim, right_dim):
    return lax.dot_general(
        left, right, (((left_dim,), (right_dim,)), ((), ())), preferred_element_type=jnp.float32
    )


def kernel(
    sections,
    count,
    head_dim,
    seg_ref,
    far_ref,
    q_ref,
    k_ref,
    v_ref,
    u_ref,
    o_ref,
    dq_ref,
    dk_ref,
    dv_ref,
    kvw,
    qb,
    gb,
    fart,
    bias,
    acc,
    snd,
    rcv,
    st,
    up_send,
    up_recv,
    fw_send,
    fw_recv,
    dn_send,
    dn_recv,
    xc_send,
    xc_recv,
    u_send,
    u_recv,
    fa_send,
    fa_recv,
    ou_send,
    ou_recv,
    lo_sem,
):
    chips = count // CORES
    heads = HEADS // CORES
    reach = count // 2 - 1
    hops = (reach + 1) // 2
    scale = 1.0 / math.sqrt(head_dim)
    sec = lax.axis_index("section")
    me = lax.axis_index("ctx")
    chip = me // CORES
    core = me % CORES
    other = 1 - core
    sibling = chip * CORES + other
    before_sec = (sec + sections - 1) % sections
    after_sec = (sec + 1) % sections
    inputs = (q_ref, k_ref, v_ref)
    results = (o_ref, dq_ref, dk_ref, dv_ref)

    def cols(h):
        return pl.ds(pl.multiple_of(h * head_dim, head_dim), head_dim)

    def half(side):
        return pl.ds(pl.multiple_of(side * (heads * head_dim), heads * head_dim), heads * head_dim)

    def rows(block, n=1):
        if isinstance(block, int):
            return pl.ds(block * BLK, n * BLK)
        return pl.ds(pl.multiple_of(block * BLK, BLK), n * BLK)

    def hop_rows(hop):
        first = reach - 2 * hop
        return rows(0, 1) if first < 0 else rows(first, 2)

    def remote(src, dst, send, recv, section, ctx):
        return pltpu.make_async_remote_copy(
            src_ref=src,
            dst_ref=dst,
            send_sem=send,
            recv_sem=recv,
            device_id=(section, ctx),
            device_id_type=MESH,
        )

    def up(h, to_core, kv, source):
        return remote(
            inputs[1 + kv].at[0, :, cols(to_core * heads + h)],
            kvw.at[kv, rows(reach - 2 + source), cols(h)],
            up_send.at[to_core, kv, h],
            up_recv.at[source, kv, h],
            sec,
            me - core + CORES + to_core,
        )

    def forward(h, hop):
        full = reach - 2 * hop >= 0
        source = rows(reach - 2 * hop + 2, 2) if full else rows(reach - 2 * hop + 3, 1)
        return remote(
            kvw.at[:, source, cols(h)],
            kvw.at[:, hop_rows(hop), cols(h)],
            fw_send.at[hop - 2, h],
            fw_recv.at[hop - 2, h],
            sec,
            me + CORES,
        )

    def down_rows(hop):
        if hop > hops:
            return rows(1, 1)
        return rows(2, 1) if hop == hops - 1 else hop_rows(hop)

    def down(h, hop):
        return remote(
            snd.at[:, down_rows(hop), cols(h)],
            rcv.at[:, down_rows(hop), cols(h)],
            dn_send.at[hop - 1, h],
            dn_recv.at[hop - 1, h],
            sec,
            me - CORES,
        )

    def swap(x, block):
        dst = qb.at[rows(block), :] if x == 0 else kvw.at[x - 1, rows(reach + block), :]
        return remote(
            inputs[x].at[0, :, half(other)], dst, xc_send.at[x], xc_recv.at[x], sec, sibling
        )

    def relay(h, to_core, source):
        return remote(
            u_ref.at[0, :, cols(to_core * heads + h)],
            gb.at[rows(source), cols(h)],
            u_send.at[to_core, h],
            u_recv.at[source, h],
            before_sec,
            me - core + to_core,
        )

    held = HEADS // count
    side = me // chips
    place = me % chips

    def spread(to_chip, slot):
        return remote(
            far_ref,
            fart.at[pl.ds(slot * held, held)],
            fa_send.at[to_chip],
            fa_recv.at[slot],
            sec,
            to_chip * CORES + side,
        )

    def give(h, x):
        return remote(
            st.at[x, rows(other), cols(h)],
            results[x].at[0, :, cols(core * heads + h)],
            ou_send.at[x, h],
            ou_recv.at[x, h],
            sec,
            sibling,
        )

    def take(h, x):
        return remote(
            st.at[x, rows(core), cols(h)],
            results[x].at[0, :, cols(other * heads + h)],
            ou_send.at[x, h],
            ou_recv.at[x, h],
            sec,
            sibling,
        )

    def own(x):
        dst = qb.at[rows(core), :] if x == 0 else kvw.at[x - 1, rows(reach + core), :]
        return pltpu.make_async_copy(inputs[x].at[0, :, half(core)], dst, lo_sem.at[x])

    def own_far():
        return pltpu.make_async_copy(far_ref, fart.at[pl.ds(place * held, held)], lo_sem.at[3])

    barrier = pltpu.get_barrier_semaphore()
    for step in range(1, count):
        pl.semaphore_signal(
            barrier, inc=1, device_id=(sec, (me + step) % count), device_id_type=MESH
        )
    for section in (before_sec, after_sec):
        for to_core in range(CORES):
            pl.semaphore_signal(
                barrier, inc=1, device_id=(section, me - core + to_core), device_id_type=MESH
            )

    for hop in range(1, hops + 1):

        @pl.when(chip < hop)
        def _():
            first = max(reach - 2 * hop, 0)
            height = (1 if reach - 2 * hop < 0 else 2) * BLK
            kvw[:, pl.ds(first * BLK, height), :] = jnp.zeros(
                (2, height, heads * head_dim), kvw.dtype
            )

    for x in range(3):
        own(x).start()

    @pl.when(side == core)
    def _():
        own_far().start()

    pl.semaphore_wait(barrier, count - 1 + 2 * CORES)

    def send_up(h):
        @pl.when(chip < chips - 1)
        def _():
            for kv in range(2):
                for to_core in range(CORES):
                    up(h, to_core, kv, core).start()

    def send_relay(h):
        for to_core in range(CORES):
            relay(h, to_core, core).start()

    for h in range(LEAD):
        send_up(h)
    for step in range(chips):

        @pl.when(jnp.logical_not(step * CORES + side == me))
        def _():
            spread(step, place).start()

    for x in range(3):
        swap(x, core).start()
    for h in range(LEAD + 1):
        send_relay(h)

    row_id = lax.broadcasted_iota(jnp.int32, (BLK, BLK), 0)
    col_id = lax.broadcasted_iota(jnp.int32, (BLK, BLK), 1)
    causal = jnp.where(col_id <= row_id, 0.0, HIDDEN).astype(jnp.float32)
    for qi in range(2):
        doc = seg_ref[0, chip * CORES + qi]
        for i in range(reach + 1):
            block = chip * CORES + qi - reach + i
            same = jnp.logical_and(block >= 0, seg_ref[0, jnp.maximum(block, 0)] == doc)
            shown = jnp.where(same, 0.0, HIDDEN).astype(jnp.float32)
            here = causal if i == reach else jnp.zeros((BLK, BLK), jnp.float32)
            bias[pl.ds(qi * BLK, BLK), pl.ds(i * BLK, BLK)] = here + shown

    for x in range(3):
        own(x).wait()
        swap(x, other).wait_recv()

    @pl.when(side == core)
    def _():
        own_far().wait()

    for step in range(chips):

        @pl.when(jnp.logical_not(core * chips + step == me))
        def _():
            spread(0, step).wait_recv()

    def compute(h):
        part = cols(h)
        weights_of, score_of, q_of, g_of = [], [], [], []
        for qi in range(2):
            q = qb[pl.ds(qi * BLK, BLK), part]
            g = gb[pl.ds(qi * BLK, BLK), part]
            keys = kvw[0, pl.ds(qi * BLK, (reach + 1) * BLK), part]
            values = kvw[1, pl.ds(qi * BLK, (reach + 1) * BLK), part]
            block = chip * CORES + qi
            far = fart[h, pl.ds(block, 1), :]
            pieces = []
            for i in range(reach + 1):
                if reach - i >= 3:
                    pieces.append(
                        jnp.where(far == block - reach + i, 0.0, HIDDEN).astype(jnp.float32)
                    )
                else:
                    pieces.append(jnp.zeros((1, BLK), jnp.float32))
            scores = dot(q, keys, 1, 1) * scale + bias[pl.ds(qi * BLK, BLK), :]
            scores = scores + jnp.concatenate(pieces, axis=1)
            row_max = jnp.max(scores, axis=-1, keepdims=True)
            raised = jnp.exp(scores - row_max)
            weights = raised * (1.0 / jnp.sum(raised, axis=-1, keepdims=True))
            low = weights.astype(jnp.bfloat16)
            attended = dot(low, values, 1, 0).astype(jnp.bfloat16)
            st[0, pl.ds(qi * BLK, BLK), part] = attended
            inner = jnp.sum(
                g.astype(jnp.float32) * attended.astype(jnp.float32), axis=-1, keepdims=True
            )
            score = (weights * (dot(g, values, 1, 1) - inner)).astype(jnp.bfloat16)
            st[1, pl.ds(qi * BLK, BLK), part] = (dot(score, keys, 1, 0) * scale).astype(
                jnp.bfloat16
            )
            weights_of.append(low)
            score_of.append(score)
            q_of.append(q)
            g_of.append(g)
        for kv, (left, right, factor) in enumerate(
            ((score_of, q_of, scale), (weights_of, g_of, 1.0))
        ):
            acc[h, kv, pl.ds(0, BLK), :] = dot(left[0][:, :BLK], right[0], 0, 0) * factor
            acc[h, kv, pl.ds((reach + 1) * BLK, BLK), :] = (
                dot(left[1][:, reach * BLK :], right[1], 0, 0) * factor
            )
            both = jnp.concatenate([left[0][:, BLK:], left[1][:, : reach * BLK]], axis=0)
            acc[h, kv, pl.ds(BLK, reach * BLK), :] = (
                dot(both, jnp.concatenate(right, axis=0), 0, 0) * factor
            )

    def hand_out(h, x):
        give(h, x).start()
        results[x][0, :, cols(core * heads + h)] = st[x, rows(core), cols(h)]

    def send_down(h, hop):
        @pl.when(chip >= (hops - 1 if hop > hops else hop))
        def _():
            for kv in range(2):
                snd[kv, down_rows(hop), cols(h)] = acc[h, kv, down_rows(hop), :].astype(
                    jnp.bfloat16
                )
            down(h, hop).start()

    def at(h, action):
        @pl.when(jnp.logical_and(h >= 0, h < heads))
        def _():
            action(h)

    def arrive(hop):
        def action(h):
            @pl.when(chip >= hop)
            def _():
                if hop == 1:
                    for source in range(CORES):
                        for kv in range(2):
                            up(h, 0, kv, source).wait_recv()
                else:
                    forward(h, hop).wait_recv()

            if hop < hops:

                @pl.when(jnp.logical_and(chip >= hop, chip < chips - 1))
                def _():
                    forward(h, hop + 1).start()

        return action

    def work(h):
        for source in range(CORES):
            relay(h, 0, source).wait_recv()
        compute(h)
        send_down(h, hops)
        if hops > 1:
            send_down(h, hops + 1)
        for x in range(2):
            hand_out(h, x)

    def settle(hop):
        def action(h):
            target = max(reach - 2 * hop + 2, 0) if reach - 2 * hop >= 0 else 2
            if reach - 2 * hop < 0:
                target = reach - 2 * hop + 3
            height = BLK if reach - 2 * hop < 0 else 2 * BLK

            @pl.when(jnp.logical_and(chip < chips - 1, chip + 1 >= hop))
            def _():
                down(h, hop).wait_recv()
                if hop == hops - 1:
                    down(h, hops + 1).wait_recv()
                for kv in range(2):
                    acc[h, kv, pl.ds(target * BLK, height), :] += rcv[
                        kv, hop_rows(hop), cols(h)
                    ].astype(jnp.float32)

            if hop > 1:
                send_down(h, hop - 1)
            else:
                for kv in range(2):
                    st[2 + kv, :, cols(h)] = acc[h, kv, pl.ds(reach * BLK, 2 * BLK), :].astype(
                        jnp.bfloat16
                    )
                    hand_out(h, 2 + kv)

        return action

    @pl.loop(0, heads + 2 * hops - 1)
    def _(i):
        @pl.when(i + LEAD < heads)
        def _():
            send_up(i + LEAD)

        @pl.when(i + LEAD + 1 < heads)
        def _():
            send_relay(i + LEAD + 1)

        for hop in range(1, hops):
            at(i - (hop - 1), arrive(hop))
        for hop in range(hops, 0, -1):
            at(i - (hops - 1) - 1 - (hops - hop), settle(hop))
        at(i - (hops - 1), arrive(hops))
        at(i - (hops - 1), work)

    for x in range(3):
        swap(x, core).wait_send()
    for step in range(chips):

        @pl.when(jnp.logical_not(step * CORES + side == me))
        def _():
            spread(step, place).wait_send()

    @pl.loop(0, heads)
    def _(h):
        @pl.when(chip < chips - 1)
        def _():
            for kv in range(2):
                for to_core in range(CORES):
                    up(h, to_core, kv, core).wait_send()

        for hop in range(2, hops + 1):

            @pl.when(jnp.logical_and(chip >= hop - 1, chip < chips - 1))
            def _():
                forward(h, hop).wait_send()

        for hop in range(1, hops + 1):

            @pl.when(chip >= hop)
            def _():
                down(h, hop).wait_send()
                if hop == hops - 1:
                    down(h, hops + 1).wait_send()

        for to_core in range(CORES):
            relay(h, to_core, core).wait_send()
        for x in range(4):
            give(h, x).wait_send()
            take(h, x).wait_recv()


def store(*refs):
    sems = refs[8]
    copies = [pltpu.make_async_copy(refs[x], refs[4 + x], sems.at[x]) for x in range(4)]
    for copy in copies:
        copy.start()
    for copy in copies:
        copy.wait()


def local(queries, key_states, value_states, upstream, layout, segments):
    sections = lax.axis_size("section")
    count = lax.axis_size("ctx")
    width = queries.shape[-1]
    head_dim = width // HEADS
    heads = HEADS // CORES
    held, blocks, _ = layout.shape[1:]
    chips = count // CORES
    reach = count // 2 - 1
    hops = (reach + 1) // 2
    plan = layout[0]
    distance = (jnp.arange(blocks, dtype=jnp.int32)[None, :, None] - plan + blocks) % blocks
    far = jnp.sum(jnp.where(distance >= 3, plan, 0), axis=-1)
    far = jnp.broadcast_to(far[:, :, None], (held, blocks, BLK)).astype(jnp.int32)
    away = pl.BlockSpec(memory_space=pl.ANY)
    vmem = pl.BlockSpec(memory_space=pltpu.VMEM)
    part = heads * head_dim
    dma = pltpu.SemaphoreType.DMA
    shapes = [jax.ShapeDtypeStruct(queries.shape, jnp.bfloat16)] * 4
    made = tuple(
        pl.pallas_call(
            functools.partial(kernel, sections, count, head_dim),
            out_shape=shapes,
            in_specs=[pl.BlockSpec(memory_space=pltpu.SMEM)] + [away] * 5,
            out_specs=[vmem] * 4,
            scratch_shapes=[
                pltpu.VMEM((2, (reach + 2) * BLK, part), jnp.bfloat16),
                pltpu.VMEM((2 * BLK, part), jnp.bfloat16),
                pltpu.VMEM((2 * BLK, part), jnp.bfloat16),
                pltpu.VMEM((heads, blocks, BLK), jnp.int32),
                pltpu.VMEM((2 * BLK, (reach + 1) * BLK), jnp.float32),
                pltpu.VMEM((heads, 2, (reach + 2) * BLK, head_dim), jnp.float32),
                pltpu.VMEM((2, reach * BLK, part), jnp.bfloat16),
                pltpu.VMEM((2, reach * BLK, part), jnp.bfloat16),
                pltpu.VMEM((4, 2 * BLK, part), jnp.bfloat16),
                dma((CORES, 2, heads)),
                dma((CORES, 2, heads)),
                dma((max(hops - 1, 1), heads)),
                dma((max(hops - 1, 1), heads)),
                dma((hops + 1, heads)),
                dma((hops + 1, heads)),
                dma((3,)),
                dma((3,)),
                dma((CORES, heads)),
                dma((CORES, heads)),
                dma((chips,)),
                dma((chips,)),
                dma((4, heads)),
                dma((4, heads)),
                dma((4,)),
            ],
            compiler_params=pltpu.CompilerParams(
                collective_id=0, has_side_effects=True, vmem_limit_bytes=56 * 1024 * 1024
            ),
        )(segments, far, queries, key_states, value_states, upstream)
    )
    return tuple(
        pl.pallas_call(
            store,
            out_shape=shapes,
            in_specs=[away] * 4,
            out_specs=[away] * 4,
            scratch_shapes=[dma((4,))],
        )(*made)
    )


def solution(mesh):
    field = P("section", "ctx", None)
    return jax.shard_map(
        local,
        mesh=mesh,
        in_specs=(field,) * 4 + (P("section", "ctx", None, None), P("section", None)),
        out_specs=(field,) * 4,
        check_vma=False,
    )
```
